32 devices in a mesh: groups: 2 (over y), row: 4 (over z), col: 4 (over x, core).
Axes of the slice: x: 2, y: 2, z: 4, core: 2. Of those that a mesh axis runs over, the one named last changes fastest.
Arguments:
- patches: bfloat16 [8, 4, 1024, 1408], P(('groups', 'row'), 'col'), parts along dimension 0, may hold values from -54 to 54
- keep_list: int32 [8, 4, 256], P(('groups', 'row'), 'col'), parts along dimension 0, may hold values from 0 to 1023, as said below
- destination: int32 [8, 4, 256], P(('groups', 'row'), 'col'), parts along dimension 0, may hold values from -1 to 255, as said below
- counts: int32 [8, 4], P('groups'), parts along dimension 0, may hold values from 64 to 256, as said below
- link_open: int32 [8, 4, 2], P('groups'), parts along dimension 0, may hold values 0 or 1
- ln_gain: float32 [1408], replicated, may hold values from 0.1 to 1.9
- w_qkv: bfloat16 [1408, 2112], replicated, may hold values from -0.15625 to 0.15625
- head_scale: float32 [8], replicated, may hold values from 1 to 4
- w_out: bfloat16 [704, 1408], replicated, may hold values from -0.4375 to 0.4375
- cotangent: bfloat16 [8, 4, 256, 1408], P(('groups', 'row'), 'col'), parts along dimension 0, may hold values from -6 to 6
Outputs:
- layer_out: bfloat16 [8, 4, 256, 1408], P(('groups', 'row'), 'col'), parts along dimension 0
- patch_grad: bfloat16 [8, 4, 256, 1408], P(('groups', 'row'), 'col'), parts along dimension 0
The draws below stay inside these ranges and needn't reach their ends.
There are 2 independent parts, one for each index of `groups`. The reference program is written for one: setup_inputs(seed, part) draws one part's arguments, and reference() takes and returns one part's arrays. A program takes and returns all parts, laid end to end along the dimension named above; an argument that names none is the same for every part. Nothing has to cross between parts.
Inputs may be any that keep to these rules, and one draw needn't show every extreme that they name: `keep_list`: within a window the entries are distinct patch indices. `counts`: some window keeps 256 tokens. destination[r, c, j] is -1 exactly where j >= counts[r, c]; elsewhere the owner along row is destination // 64 and the position in the window's block is destination % 64; entries of one window are distinct, so a window sends at most 64 tokens to one owner, and in every column some owner receives 64 tokens from every window.
All inputs are finite; a program needn't handle non-finite values.
Results may differ from the reference program's by a relative error of at most 0.012.
The reference program's roundings to bfloat16 on the way count: a program that leaves them out, or rounds other values in their place, can miss the bound.
Values may be sent and summed in bfloat16 or wider, within the bound.
A program may use at most 128 MiB of HBM per device.

```python
import math
import jax
import jax.numpy as jnp
from jax import lax

D = 1408
HEADS = 8
HEAD_DIM = 88
PATCHES = 1024
KEEP = 256
ATTN_WIDTH = 704
SLOT_CAP = 64
GRID_ROWS = 4
GRID_COLS = 4


def window_layout(key):
    key_count, key_full, key_owner, key_order, key_mix = jax.random.split(key, 5)
    counts = jax.random.randint(key_count, (GRID_ROWS, GRID_COLS), KEEP // 4, KEEP + 1)
    chosen = jax.random.randint(key_full, (), 0, GRID_ROWS * GRID_COLS)
    counts = counts.reshape(-1).at[chosen].set(KEEP).reshape(GRID_ROWS, GRID_COLS).astype(jnp.int32)
    favoured = jax.random.randint(key_owner, (GRID_COLS,), 0, GRID_ROWS)
    slot_ids = jnp.arange(KEEP, dtype=jnp.int32)
    owner_ids = slot_ids // SLOT_CAP
    noise = jax.random.randint(key_order, (GRID_ROWS, GRID_COLS, KEEP), 0, 2 ** 18)
    priority = noise * KEEP + slot_ids + jnp.where(owner_ids[None, None, :] == favoured[None, :, None], 0, 2 ** 29)
    ordered = jnp.argsort(priority, axis=-1).astype(jnp.int32)
    mixing = jax.random.randint(key_mix, (GRID_ROWS, GRID_COLS, KEEP), 0, 2 ** 18)
    live_slot = slot_ids[None, None, :] < counts[:, :, None]
    shuffle = jnp.argsort(jnp.where(live_slot, mixing * KEEP + slot_ids, 2 ** 29 + slot_ids), axis=-1)
    placed = jnp.take_along_axis(ordered, shuffle, axis=-1)
    destination = jnp.where(live_slot, placed, -1).astype(jnp.int32)
    return (counts, destination)


def draw_counts(key, part):
    return window_layout(jax.random.fold_in(key, 17))[0]


def draw_destination(key, part):
    return window_layout(jax.random.fold_in(key, 17))[1]


def draw_keep_list(key, part):
    noise = jax.random.randint(key, (GRID_ROWS, GRID_COLS, PATCHES), 0, 2 ** 18)
    ordered = jnp.argsort(noise * PATCHES + jnp.arange(PATCHES, dtype=jnp.int32), axis=-1)
    return ordered[..., :KEEP].astype(jnp.int32)


def draw_patches(key, part):
    key_base, key_rows, key_cols = jax.random.split(key, 3)
    shape = (GRID_ROWS, GRID_COLS, PATCHES, D)
    row_scale = jnp.exp(jax.random.uniform(key_rows, (GRID_ROWS, GRID_COLS, PATCHES, 1), jnp.float32, math.log(0.3), math.log(3.0)))
    base = jax.random.truncated_normal(key_base, -6.0, 6.0, shape, jnp.float32)
    col_scale = jnp.exp(jax.random.uniform(key_cols, (D,), jnp.float32, math.log(0.3), math.log(3.0)))
    return (base * row_scale * col_scale).astype(jnp.bfloat16)


def touch_ends(array, stream_key, low, top_value):
    longest = array.shape.index(max(array.shape))
    spots = []
    for shift in (0, 1):
        where = [jax.random.randint(jax.random.fold_in(stream_key, axis), (), 0, length) for axis, length in enumerate(array.shape)]
        where[longest] = (where[longest] + shift) % array.shape[longest]
        spots.append(tuple(where))
    return array.at[spots[0]].set(low).at[spots[1]].set(top_value)


def steps_of(key, extent, pieces, smallest, high):
    gain, own = 1.0, jax.random.fold_in(key, 6)
    for dim, parts in pieces:
        heights = jnp.exp(jax.random.uniform(jax.random.fold_in(own, dim), (parts,), jnp.float32, smallest / len(pieces), high / len(pieces)))
        gain = gain * jnp.repeat(heights, extent[dim] // parts).reshape([-1 if axis == dim else 1 for axis in range(len(extent))])
    return gain


def normal_values(key, shape, scale, limit, cuts=(), kind=jnp.bfloat16):
    array = jax.random.normal(key, shape, jnp.float32) * scale
    if len(cuts) > 0:
        array = steps_of(key, shape, cuts, -0.22, 0.18) * array
    return jnp.clip(array, min=-limit, max=limit).astype(kind)


def setup_inputs(seed: int = 0, part: int = 0) -> dict:
    arg_keys = jax.random.split(jax.random.key(seed), 11)
    part_keys = jax.random.split(jax.random.fold_in(arg_keys[10], part), 11)
    patches = draw_patches(jax.random.fold_in(jax.random.fold_in(arg_keys[10], part), 71), part)
    keep_list = draw_keep_list(jax.random.fold_in(jax.random.fold_in(arg_keys[10], part), 71), part)
    destination = draw_destination(jax.random.fold_in(jax.random.fold_in(arg_keys[10], part), 71), part)
    counts = draw_counts(jax.random.fold_in(jax.random.fold_in(arg_keys[10], part), 71), part)
    link_open = touch_ends((jax.random.randint(part_keys[4], (GRID_ROWS, GRID_COLS, 2), 0, 4) < 3).astype(jnp.int32), jax.random.fold_in(part_keys[4], 1), 0, 1)
    ln_gain = jnp.clip(1.0 + 0.18 * jax.random.normal(arg_keys[5], (D,), jnp.float32), 0.1, 1.9)
    w_qkv = normal_values(arg_keys[6], (D, 3 * ATTN_WIDTH), D ** -0.5, 0.15625)
    head_scale = jnp.clip(jnp.exp(jax.random.uniform(arg_keys[7], (HEADS,), jnp.float32, math.log(1.0), math.log(4.0))), 1.0, 4.0)
    w_out = normal_values(arg_keys[8], (ATTN_WIDTH, D), (ATTN_WIDTH // 4) ** -0.5, 0.4375)
    cotangent = normal_values(part_keys[9], (GRID_ROWS, GRID_COLS, KEEP, D), 1.0, 6.0, ((0, 4), (1, 4)))
    return {"patches": patches, "keep_list": keep_list, "destination": destination, "counts": counts, "link_open": link_open, "ln_gain": ln_gain, "w_qkv": w_qkv, "head_scale": head_scale, "w_out": w_out, "cotangent": cotangent}


NEIGHBOUR_OFFSETS = ((0, 0), (-1, 0), (1, 0), (0, -1), (0, 1))

def layer_norm(kept_rows, ln_gain):
    values = kept_rows.astype(jnp.float32)
    center = lax.optimization_barrier(jnp.mean(values, axis=-1, keepdims=True))
    centred = values - center
    spread = lax.optimization_barrier(jnp.mean(centred * centred, axis=-1, keepdims=True))
    inv_std = lax.rsqrt(spread + 1e-06)
    scaled = centred * inv_std
    return ((scaled * ln_gain).astype(jnp.bfloat16), scaled, inv_std)

def head_norm(raw_rows):
    row_count = raw_rows.shape[0]
    split_heads = raw_rows.reshape(row_count, HEADS, HEAD_DIM)
    inv_rms = lax.rsqrt(lax.optimization_barrier(jnp.mean(split_heads * split_heads, axis=-1, keepdims=True)) + 1e-06)
    return ((split_heads * inv_rms).astype(jnp.bfloat16), split_heads, inv_rms)

def head_norm_back(split_heads, inv_rms, upstream):
    inner_mean = lax.optimization_barrier(jnp.mean(upstream * split_heads, axis=-1, keepdims=True))
    return inv_rms * (upstream - split_heads * inv_rms * inv_rms * inner_mean)

def attend(queries, key_rows, value_rows, key_valid, score_coef):
    scores = jnp.einsum('qhe,khe->hqk', queries.astype(jnp.float32), key_rows.astype(jnp.float32)) * score_coef[:, None, None]
    raised = jnp.where(key_valid[None, None, :], jnp.exp(scores), 0.0)
    total_sum = lax.optimization_barrier(jnp.sum(raised, axis=-1, keepdims=True))
    weights = raised / total_sum
    rounded = weights.astype(jnp.bfloat16)
    attended = jnp.einsum('hqk,khe->qhe', rounded.astype(jnp.float32), value_rows.astype(jnp.float32))
    return (attended.astype(jnp.bfloat16), weights, rounded)

def score_back(weights, value_rows, out_grad):
    dot_grad = jnp.einsum('qhe,khe->hqk', out_grad.astype(jnp.float32), value_rows.astype(jnp.float32))
    row_delta = lax.optimization_barrier(jnp.sum(weights * dot_grad, axis=-1, keepdims=True))
    return (weights * (dot_grad - row_delta)).astype(jnp.bfloat16)

def query_back(score_grad, key_rows, score_coef):
    return jnp.einsum('hqk,khe->qhe', score_grad.astype(jnp.float32), key_rows.astype(jnp.float32)) * score_coef[None, :, None]

def key_back(score_grad, rounded, queries, out_grad, score_coef):
    key_part = jnp.einsum('hqk,qhe->khe', score_grad.astype(jnp.float32), queries.astype(jnp.float32)) * score_coef[None, :, None]
    value_part = jnp.einsum('hqk,qhe->khe', rounded.astype(jnp.float32), out_grad.astype(jnp.float32))
    return (key_part, value_part)

def reference(patches, keep_list, destination, counts, link_open, ln_gain, w_qkv, head_scale, w_out, cotangent):
    token_total = GRID_ROWS * GRID_COLS * KEEP
    width = ATTN_WIDTH
    kept_rows = jax.vmap(jax.vmap(lambda tile_rows, picks: tile_rows[picks]))(patches, keep_list)
    flat_kept = kept_rows.reshape(token_total, D)
    normed, scaled, inv_std = layer_norm(flat_kept, ln_gain)
    projected = jnp.dot(normed, w_qkv, preferred_element_type=jnp.float32)
    query_norm, query_split, query_rms = head_norm(projected[:, :width])
    key_norm, key_split, key_rms = head_norm(projected[:, width:2 * width])
    value_flat = projected[:, 2 * width:].astype(jnp.bfloat16).reshape(token_total, HEADS, HEAD_DIM)
    score_coef = head_scale / math.sqrt(HEAD_DIM)
    grid_shape = (GRID_ROWS, GRID_COLS, KEEP, HEADS, HEAD_DIM)
    query_grid = query_norm.reshape(grid_shape)
    padding = ((1, 1), (1, 1), (0, 0), (0, 0), (0, 0))
    key_pad = jnp.pad(key_norm.reshape(grid_shape), padding)
    value_pad = jnp.pad(value_flat.reshape(grid_shape), padding)
    count_pad = jnp.pad(counts, 1)
    link_pad = jnp.pad(link_open, ((1, 1), (1, 1), (0, 0)))
    row_ids = jnp.arange(GRID_ROWS)[:, None]
    col_ids = jnp.arange(GRID_COLS)[None, :]
    open_flags = jnp.stack([jnp.ones((GRID_ROWS, GRID_COLS), jnp.bool_), link_pad[:GRID_ROWS, 1:GRID_COLS + 1, 1] == 1, (link_open[:, :, 1] == 1) & (row_ids < GRID_ROWS - 1), link_pad[1:GRID_ROWS + 1, :GRID_COLS, 0] == 1, (link_open[:, :, 0] == 1) & (col_ids < GRID_COLS - 1)], axis=-1)
    live_slot = destination >= 0
    safe_slot = jnp.maximum(destination, 0)
    owner_row = safe_slot // SLOT_CAP
    row_grid = jnp.broadcast_to(jnp.arange(GRID_ROWS)[:, None, None], destination.shape)
    col_grid = jnp.broadcast_to(jnp.arange(GRID_COLS)[None, :, None], destination.shape)
    packed_slot = row_grid * SLOT_CAP + safe_slot % SLOT_CAP
    token_grad = jnp.where(live_slot[..., None], cotangent[owner_row, col_grid, packed_slot], 0.0).astype(jnp.bfloat16)
    out_grad = jnp.dot(token_grad.reshape(token_total, D), w_out.T, preferred_element_type=jnp.float32).astype(jnp.bfloat16).reshape(grid_shape)
    position = jnp.arange(KEEP)

    def window_step(window_at, state_all):
        attended_all, query_all, key_acc, value_acc = state_all
        row_at = window_at // GRID_COLS
        col_at = window_at % GRID_COLS
        key_list = []
        value_list = []
        valid_list = []
        for panel_at, (shift_row, shift_col) in enumerate(NEIGHBOUR_OFFSETS):
            key_list.append(key_pad[row_at + 1 + shift_row, col_at + 1 + shift_col])
            value_list.append(value_pad[row_at + 1 + shift_row, col_at + 1 + shift_col])
            valid_list.append((position < count_pad[row_at + 1 + shift_row, col_at + 1 + shift_col]) & open_flags[row_at, col_at, panel_at])
        key_rows = jnp.concatenate(key_list, axis=0)
        value_rows = jnp.concatenate(value_list, axis=0)
        key_valid = jnp.concatenate(valid_list, axis=0)
        queries = query_grid[row_at, col_at]
        window_grad = out_grad[row_at, col_at]
        attended, weights, rounded = attend(queries, key_rows, value_rows, key_valid, score_coef)
        score_grad = score_back(weights, value_rows, window_grad)
        query_part = query_back(score_grad, key_rows, score_coef)
        key_part, value_part = key_back(score_grad, rounded, queries, window_grad, score_coef)
        attended_all = attended_all.at[window_at].set(attended)
        query_all = query_all.at[window_at].set(query_part)
        for panel_at, (shift_row, shift_col) in enumerate(NEIGHBOUR_OFFSETS):
            key_acc = key_acc.at[row_at + 1 + shift_row, col_at + 1 + shift_col].add(key_part[panel_at * KEEP:(panel_at + 1) * KEEP])
            value_acc = value_acc.at[row_at + 1 + shift_row, col_at + 1 + shift_col].add(value_part[panel_at * KEEP:(panel_at + 1) * KEEP])
        return (attended_all, query_all, key_acc, value_acc)
    window_total = GRID_ROWS * GRID_COLS
    pad_shape = (GRID_ROWS + 2, GRID_COLS + 2, KEEP, HEADS, HEAD_DIM)
    start_state = (jnp.zeros((window_total, KEEP, HEADS, HEAD_DIM), jnp.bfloat16), jnp.zeros((window_total, KEEP, HEADS, HEAD_DIM), jnp.float32), jnp.zeros(pad_shape, jnp.float32), jnp.zeros(pad_shape, jnp.float32))
    attended_all, query_all, key_acc, value_acc = lax.fori_loop(0, window_total, window_step, start_state)
    kept_out = (flat_kept.astype(jnp.float32) + jnp.dot(attended_all.reshape(token_total, width), w_out, preferred_element_type=jnp.float32)).astype(jnp.bfloat16)
    target_row = jnp.where(live_slot, owner_row, GRID_ROWS)
    layer_out = jnp.zeros((GRID_ROWS, GRID_COLS, KEEP, D), jnp.bfloat16)
    layer_out = layer_out.at[target_row, col_grid, packed_slot].set(kept_out.reshape(GRID_ROWS, GRID_COLS, KEEP, D), mode='drop')
    key_total = key_acc[1:-1, 1:-1].reshape(token_total, HEADS, HEAD_DIM)
    value_total = value_acc[1:-1, 1:-1].reshape(token_total, width)
    query_pre = head_norm_back(query_split, query_rms, query_all.reshape(token_total, HEADS, HEAD_DIM))
    key_pre = head_norm_back(key_split, key_rms, key_total)
    proj_grad = jnp.concatenate([query_pre.reshape(token_total, width), key_pre.reshape(token_total, width), value_total], axis=1).astype(jnp.bfloat16)
    normed_grad = jnp.dot(proj_grad, w_qkv.T, preferred_element_type=jnp.float32)
    gained = normed_grad * ln_gain
    back_norm = inv_std * (gained - lax.optimization_barrier(jnp.mean(gained, axis=-1, keepdims=True)) - scaled * lax.optimization_barrier(jnp.mean(gained * scaled, axis=-1, keepdims=True)))
    patch_grad = (token_grad.reshape(token_total, D).astype(jnp.float32) + back_norm).astype(jnp.bfloat16)
    return (layer_out, patch_grad.reshape(GRID_ROWS, GRID_COLS, KEEP, D))
```

```python
import functools
import math

import jax
import jax.numpy as jnp
from jax import lax
from jax.experimental import pallas as pl
from jax.experimental.pallas import tpu as pltpu
from jax.sharding import PartitionSpec as P

MESH = pl.DeviceIdType.MESH
BF16 = jnp.bfloat16
F32 = jnp.float32
LANES = 128
NN = (((1,), (0,)), ((), ()))
NT = (((1,), (1,)), ((), ()))
TN = (((0,), (0,)), ((), ()))


def dot(a, b, dims):
    return lax.dot_general(a, b, dims, preferred_element_type=F32)


def tiles(total, step=256):
    return [(at, min(step, total - at)) for at in range(0, total, step)]


def kernel(
    sizes,
    patches_hbm, keep_ref, dest_ref, counts_ref, link_ref, gain_ref, wqkv_hbm, scale_ref, wout_hbm,
    cot_hbm,
    layer_hbm, grad_hbm,
    patches, wqkv, wout, incoming, kept, token, scaled, inv_std, normed, proj, raw, rms, qh, doh, kvh,
    kv_send, kv_far, exps, dps, att_t, own_dkv, far_dkv, dkv_send, dkv_far, pgh, pg, outgoing, grad_out,
    load_sem, cot_send_sem, cot_recv_sem, kv_send_sem, kv_recv_sem, dkv_send_sem, dkv_recv_sem,
    out_send_sem, out_recv_sem, own_sem,
):
    rows, cols, keep, depth, patch_count, heads, hd = sizes
    cap = keep // rows
    group = lax.axis_index("groups")
    row = lax.axis_index("row")
    col = lax.axis_index("col")

    loads = [
        pltpu.make_async_copy(patches_hbm, patches, load_sem.at[0]),
        pltpu.make_async_copy(wqkv_hbm, wqkv, load_sem.at[1]),
        pltpu.make_async_copy(wout_hbm, wout, load_sem.at[2]),
    ]
    for load in loads:
        load.start()

    near = [
        (row > 0, (group, row - 1, col)),
        (row < rows - 1, (group, row + 1, col)),
        (col > 0, (group, row, col - 1)),
        (col < cols - 1, (group, row, col + 1)),
    ]
    opposite = [1, 0, 3, 2]
    peers = [lax.rem(row + shift, rows) for shift in range(rows)]

    barrier = pltpu.get_barrier_semaphore()
    for shift in range(1, rows):
        pl.semaphore_signal(
            barrier, inc=1, device_id=(group, peers[shift], col), device_id_type=MESH
        )
    for exists, target in near[2:]:

        @pl.when(exists)
        def _():
            pl.semaphore_signal(barrier, inc=1, device_id=target, device_id_type=MESH)

    beside = jnp.where(col > 0, 1, 0) + jnp.where(col < cols - 1, 1, 0)
    pl.semaphore_wait(barrier, rows - 1 + beside)

    def block_of(index):
        return pl.ds(pl.multiple_of(index * cap, cap), cap)

    cot_copies = [
        pltpu.make_async_remote_copy(
            src_ref=cot_hbm.at[block_of(peers[shift])],
            dst_ref=incoming.at[block_of(row)],
            send_sem=cot_send_sem.at[shift],
            recv_sem=cot_recv_sem.at[shift],
            device_id=(group, peers[shift], col),
            device_id_type=MESH,
        )
        for shift in range(1, rows)
    ]
    for copy in cot_copies:
        copy.start()
    own_cot = pltpu.make_async_copy(
        cot_hbm.at[block_of(row)], incoming.at[block_of(row)], own_sem.at[0]
    )
    own_cot.start()

    for side, (exists, _) in enumerate(near):

        @pl.when(jnp.logical_not(exists))
        def _():
            kv_far[side] = jnp.zeros(kv_far.shape[1:], BF16)
            dkv_far[side] = jnp.zeros(dkv_far.shape[1:], BF16)

    pick = (
        lax.broadcasted_iota(jnp.int32, (patch_count, keep), 0) == keep_ref[...]
    ).astype(F32).astype(BF16)
    loads[0].wait()
    for at, size in tiles(depth):
        kept[:, at : at + size] = dot(pick, patches[:, at : at + size], TN).astype(BF16)

    values = kept[...].astype(F32)
    centred = values - jnp.mean(values, axis=-1, keepdims=True)
    inv = lax.rsqrt(jnp.mean(centred * centred, axis=-1, keepdims=True) + 1e-06)
    inv_std[...] = inv
    scaled[...] = centred * inv
    normed[...] = (scaled[...] * gain_ref[...]).astype(BF16)

    loads[1].wait()
    for at, size in tiles(3 * heads * hd):
        proj[:, at : at + size] = dot(normed[...], wqkv[:, at : at + size], NN)

    pieces = [None] * (2 * heads)
    for piece in range(3 * heads):
        part = proj[:, piece * hd : (piece + 1) * hd]
        if piece < 2 * heads:
            mean = jnp.sum(part * part, axis=-1, keepdims=True) * (1.0 / hd)
            inv = lax.rsqrt(mean + 1e-06)
            raw[piece, :, :hd] = part
            rms[piece] = inv
            part = (part * inv).astype(BF16)
        else:
            part = part.astype(BF16)
        if piece < heads:
            qh[piece] = jnp.zeros(qh.shape[1:], BF16)
            qh[piece, :, :hd] = part
        else:
            which, head = divmod(piece - heads, heads)
            pieces[2 * head + which] = part
            kvh[0, 2 * head + which] = jnp.zeros(kvh.shape[2:], BF16)
            kvh[0, 2 * head + which, :, :hd] = part
    kv_send[...] = jnp.concatenate(pieces, axis=1)

    kv_copies = []
    for side, (exists, target) in enumerate(near):
        copy = pltpu.make_async_remote_copy(
            src_ref=kv_send,
            dst_ref=kv_far.at[opposite[side]],
            send_sem=kv_send_sem.at[side],
            recv_sem=kv_recv_sem.at[opposite[side]],
            device_id=target,
            device_id_type=MESH,
        )
        kv_copies.append(copy)

        @pl.when(exists)
        def _():
            copy.start()

    slot_pick = (
        lax.broadcasted_iota(jnp.int32, (keep, keep), 0) == dest_ref[...]
    ).astype(F32).astype(BF16)
    for copy in cot_copies:
        copy.wait()
    own_cot.wait()
    for at, size in tiles(depth):
        token[:, at : at + size] = dot(slot_pick, incoming[:, at : at + size], TN).astype(BF16)
    loads[2].wait()
    out_grad = dot(token[...], wout[...], NT).astype(BF16)
    for head in range(heads):
        doh[head] = jnp.zeros(doh.shape[1:], BF16)
        doh[head, :, :hd] = out_grad[:, head * hd : (head + 1) * hd]

    above_row = jnp.maximum(row - 1, 0)
    below_row = jnp.minimum(row + 1, rows - 1)
    left_col = jnp.maximum(col - 1, 0)
    right_col = jnp.minimum(col + 1, cols - 1)
    limits = [
        counts_ref[row, col],
        jnp.where(row > 0, counts_ref[above_row, col] * link_ref[above_row, col, 1], 0),
        jnp.where(row < rows - 1, counts_ref[below_row, col] * link_ref[row, col, 1], 0),
        jnp.where(col > 0, counts_ref[row, left_col] * link_ref[row, left_col, 0], 0),
        jnp.where(col < cols - 1, counts_ref[row, right_col] * link_ref[row, col, 0], 0),
    ]

    for side, (exists, _) in enumerate(near):

        @pl.when(exists)
        def _():
            kv_copies[side].wait_send()
            pltpu.make_async_remote_copy(
                src_ref=kv_send,
                dst_ref=kv_far.at[side],
                send_sem=kv_send_sem.at[side],
                recv_sem=kv_recv_sem.at[side],
                device_id=near[side][1],
                device_id_type=MESH,
            ).wait_recv()

        far = kv_far[side]
        for piece in range(2 * heads):
            kvh[1 + side, piece] = jnp.zeros(kvh.shape[2:], BF16)
            kvh[1 + side, piece, :, :hd] = far[:, piece * hd : (piece + 1) * hd]

    panels = 5
    key_at = lax.broadcasted_iota(jnp.int32, (keep, keep), 0)

    def head_step(head, carry):
        coef = scale_ref[head] * (1.0 / math.sqrt(hd))
        query = qh[head]
        grad = doh[head]
        total = jnp.zeros((1, keep), F32)
        for panel in range(panels):
            scores = dot(kvh[panel, 2 * head], query, NT) * coef
            raised = jnp.where(key_at < limits[panel], jnp.exp(scores), 0.0)
            total = total + jnp.sum(raised, axis=0, keepdims=True)
            exps[panel] = raised
        inverse = 1.0 / total
        delta = jnp.zeros((1, keep), F32)
        attended = jnp.zeros((LANES, keep), F32)
        for panel in range(panels):
            value = kvh[panel, 2 * head + 1]
            weights = exps[panel] * inverse
            exps[panel] = weights
            rounded = weights.astype(BF16)
            attended = attended + dot(value, rounded, TN)
            dot_grad = dot(value, grad, NT)
            dps[panel] = dot_grad
            delta = delta + jnp.sum(weights * dot_grad, axis=0, keepdims=True)
            value_grad = dot(rounded, grad, NN)
            if panel == 0:
                own_dkv[2 * head + 1] = value_grad
            else:
                far_dkv[panel - 1, 2 * head + 1] = value_grad.astype(BF16)
        att_t[pl.ds(pl.multiple_of(head * hd, 8), hd), :] = attended[:hd]
        query_grad = jnp.zeros((LANES, keep), F32)
        for panel in range(panels):
            score_grad = (exps[panel] * (dps[panel] - delta)).astype(BF16)
            query_grad = query_grad + dot(kvh[panel, 2 * head], score_grad, TN)
            key_grad = dot(score_grad, query, NN) * coef
            if panel == 0:
                own_dkv[2 * head] = key_grad
            else:
                far_dkv[panel - 1, 2 * head] = key_grad.astype(BF16)
        upstream = query_grad.T[:, :hd] * coef
        split = raw[head, :, :hd]
        inv = rms[head]
        inner = jnp.sum(upstream * split, axis=-1, keepdims=True) * (1.0 / hd)
        pgh[head, :, :hd] = (inv * (upstream - split * (inv * inv * inner))).astype(BF16)
        return carry

    lax.fori_loop(0, heads, head_step, 0)

    dkv_copies = []
    for side, (exists, target) in enumerate(near):
        dkv_send[side] = jnp.concatenate(
            [far_dkv[side, piece, :, :hd] for piece in range(2 * heads)], axis=1
        )
        copy = pltpu.make_async_remote_copy(
            src_ref=dkv_send.at[side],
            dst_ref=dkv_far.at[opposite[side]],
            send_sem=dkv_send_sem.at[side],
            recv_sem=dkv_recv_sem.at[opposite[side]],
            device_id=target,
            device_id_type=MESH,
        )
        dkv_copies.append(copy)

        @pl.when(exists)
        def _():
            copy.start()

    attended = att_t[...].astype(BF16)
    for at, size in tiles(depth):
        span = slice(at, at + size)
        kept_out = (kept[:, span].astype(F32) + dot(attended, wout[:, span], TN)).astype(BF16)
        outgoing[:, span] = dot(slot_pick, kept_out, NN).astype(BF16)
    out_copies = [
        pltpu.make_async_remote_copy(
            src_ref=outgoing.at[block_of(peers[shift])],
            dst_ref=layer_hbm.at[block_of(row)],
            send_sem=out_send_sem.at[shift],
            recv_sem=out_recv_sem.at[shift],
            device_id=(group, peers[shift], col),
            device_id_type=MESH,
        )
        for shift in range(1, rows)
    ]
    for copy in out_copies:
        copy.start()
    own_out = pltpu.make_async_copy(
        outgoing.at[block_of(row)], layer_hbm.at[block_of(row)], own_sem.at[1]
    )
    own_out.start()

    for side, (exists, target) in enumerate(near):

        @pl.when(exists)
        def _():
            dkv_copies[side].wait_send()
            pltpu.make_async_remote_copy(
                src_ref=dkv_send.at[side],
                dst_ref=dkv_far.at[side],
                send_sem=dkv_send_sem.at[side],
                recv_sem=dkv_recv_sem.at[side],
                device_id=target,
                device_id_type=MESH,
            ).wait_recv()

    for head in range(heads):
        for which in range(2):
            piece = 2 * head + which
            span = slice(piece * hd, (piece + 1) * hd)
            upstream = own_dkv[piece, :, :hd]
            for side in range(4):
                upstream = upstream + dkv_far[side, :, span].astype(F32)
            if which == 0:
                split = raw[heads + head, :, :hd]
                inv = rms[heads + head]
                inner = jnp.sum(upstream * split, axis=-1, keepdims=True) * (1.0 / hd)
                upstream = inv * (upstream - split * (inv * inv * inner))
            pgh[heads * (1 + which) + head, :, :hd] = upstream.astype(BF16)
    pg[...] = jnp.concatenate([pgh[piece, :, :hd] for piece in range(3 * heads)], axis=1)

    gained = proj
    for at, size in tiles(depth):
        span = slice(at, at + size)
        gained[:, span] = dot(pg[...], wqkv[span, :], NT) * gain_ref[:, span]
    grads = gained[:, :depth]
    mean_grad = jnp.mean(grads, axis=-1, keepdims=True)
    mean_scaled = jnp.mean(grads * scaled[...], axis=-1, keepdims=True)
    grad_out[...] = (
        token[...].astype(F32) + inv_std[...] * (grads - mean_grad - scaled[...] * mean_scaled)
    ).astype(BF16)
    store = pltpu.make_async_copy(grad_out, grad_hbm, own_sem.at[2])
    store.start()
    for copy in out_copies:
        copy.wait()
    own_out.wait()
    store.wait()


def per_device(
    rows, cols,
    patches, keep_list, destination, counts, link_open, ln_gain, w_qkv, head_scale, w_out, cotangent,
):
    keep = keep_list.shape[2]
    patch_count, depth = patches.shape[2:]
    heads = head_scale.shape[0]
    width = w_out.shape[0]
    hd = width // heads
    sizes = (rows, cols, keep, depth, patch_count, heads, hd)
    hbm = pl.BlockSpec(memory_space=pl.ANY)
    vmem = pl.BlockSpec(memory_space=pltpu.VMEM)
    smem = pl.BlockSpec(memory_space=pltpu.SMEM)
    dma = pltpu.SemaphoreType.DMA
    scratch = [
        pltpu.VMEM((patch_count, depth), BF16),
        pltpu.VMEM((depth, 3 * width), BF16),
        pltpu.VMEM((width, depth), BF16),
        pltpu.VMEM((keep, depth), BF16),
        pltpu.VMEM((keep, depth), BF16),
        pltpu.VMEM((keep, depth), BF16),
        pltpu.VMEM((keep, depth), F32),
        pltpu.VMEM((keep, 1), F32),
        pltpu.VMEM((keep, depth), BF16),
        pltpu.VMEM((keep, 3 * width), F32),
        pltpu.VMEM((2 * heads, keep, LANES), F32),
        pltpu.VMEM((2 * heads, keep, 1), F32),
        pltpu.VMEM((heads, keep, LANES), BF16),
        pltpu.VMEM((heads, keep, LANES), BF16),
        pltpu.VMEM((5, 2 * heads, keep, LANES), BF16),
        pltpu.VMEM((keep, 2 * width), BF16),
        pltpu.VMEM((4, keep, 2 * width), BF16),
        pltpu.VMEM((5, keep, keep), F32),
        pltpu.VMEM((5, keep, keep), F32),
        pltpu.VMEM((width, keep), F32),
        pltpu.VMEM((2 * heads, keep, LANES), F32),
        pltpu.VMEM((4, 2 * heads, keep, LANES), BF16),
        pltpu.VMEM((4, keep, 2 * width), BF16),
        pltpu.VMEM((4, keep, 2 * width), BF16),
        pltpu.VMEM((3 * heads, keep, LANES), BF16),
        pltpu.VMEM((keep, 3 * width), BF16),
        pltpu.VMEM((keep, depth), BF16),
        pltpu.VMEM((keep, depth), BF16),
        dma((3,)),
        dma((rows,)),
        dma((rows,)),
        dma((4,)),
        dma((4,)),
        dma((4,)),
        dma((4,)),
        dma((rows,)),
        dma((rows,)),
        dma((3,)),
    ]
    layer_out, patch_grad = pl.pallas_call(
        functools.partial(kernel, sizes),
        out_shape=(
            jax.ShapeDtypeStruct((keep, depth), BF16),
            jax.ShapeDtypeStruct((keep, depth), BF16),
        ),
        in_specs=[hbm, vmem, vmem, smem, smem, vmem, hbm, smem, hbm, hbm],
        out_specs=(hbm, hbm),
        scratch_shapes=scratch,
        compiler_params=pltpu.CompilerParams(
            collective_id=0, has_side_effects=True, vmem_limit_bytes=60 * 2**20
        ),
    )(
        patches[0, 0], keep_list[0], destination[0], counts, link_open, ln_gain[None], w_qkv,
        head_scale, w_out, cotangent[0, 0],
    )
    return (layer_out[None, None], patch_grad[None, None])


def solution(mesh):
    window = P(("groups", "row"), "col", None, None)
    slots = P(("groups", "row"), "col", None)
    placed = (
        window, slots, slots, P("groups", None), P("groups", None, None), P(), P(), P(), P(), window,
    )
    return jax.shard_map(
        functools.partial(per_device, mesh.shape["row"], mesh.shape["col"]),
        mesh=mesh,
        in_specs=placed,
        out_specs=(window, window),
        check_vma=False,
    )
```

```python
import functools
import math

import jax
import jax.numpy as jnp
from jax import lax
from jax.experimental import pallas as pl
from jax.experimental.pallas import tpu as pltpu
from jax.sharding import PartitionSpec as P

MESH = pl.DeviceIdType.MESH
BF16 = jnp.bfloat16
F32 = jnp.float32
LANES = 128
NN = (((1,), (0,)), ((), ()))
NT = (((1,), (1,)), ((), ()))
TN = (((0,), (0,)), ((), ()))


def dot(a, b, dims):
    return lax.dot_general(a, b, dims, preferred_element_type=F32)


PARTS = 2


def cuts(heads, hd, up):
    ends = [0]
    for part in range(1, PARTS + 1):
        columns = 2 * hd * (heads * part // PARTS)
        if part < PARTS:
            columns = (columns + (LANES - 1 if up else 0)) // LANES * LANES
        ends.append(columns)
    return list(zip(ends[:-1], ends[1:]))


def tiles(total, step=256):
    return [(at, min(step, total - at)) for at in range(0, total, step)]


def kernel(
    sizes,
    patches_hbm, keep_ref, dest_ref, counts_ref, link_ref, gain_ref, wqkv_hbm, scale_ref, wout_hbm,
    cot_hbm,
    layer_hbm, grad_hbm,
    patches, wqkv, wout, incoming, kept, token, scaled, inv_std, normed, proj, raw, rms, qh, doh, kvh,
    kv_send, kv_far, exps, dps, att_t, own_dkv, far_dkv, dkv_send, dkv_far, pgh, pg, outgoing, grad_out,
    load_sem, cot_send_sem, cot_recv_sem, kv_send_sem, kv_recv_sem, dkv_send_sem, dkv_recv_sem,
    out_send_sem, out_recv_sem, own_sem,
):
    rows, cols, keep, depth, patch_count, heads, hd = sizes
    cap = keep // rows
    group = lax.axis_index("groups")
    row = lax.axis_index("row")
    col = lax.axis_index("col")

    loads = [
        pltpu.make_async_copy(patches_hbm, patches, load_sem.at[0]),
        pltpu.make_async_copy(wqkv_hbm, wqkv, load_sem.at[1]),
        pltpu.make_async_copy(wout_hbm, wout, load_sem.at[2]),
    ]
    for load in loads:
        load.start()

    near = [
        (row > 0, (group, row - 1, col)),
        (row < rows - 1, (group, row + 1, col)),
        (col > 0, (group, row, col - 1)),
        (col < cols - 1, (group, row, col + 1)),
    ]
    opposite = [1, 0, 3, 2]
    peers = [lax.rem(row + shift, rows) for shift in range(rows)]

    barrier = pltpu.get_barrier_semaphore()
    for shift in range(1, rows):
        pl.semaphore_signal(
            barrier, inc=1, device_id=(group, peers[shift], col), device_id_type=MESH
        )
    for exists, target in near[2:]:

        @pl.when(exists)
        def _():
            pl.semaphore_signal(barrier, inc=1, device_id=target, device_id_type=MESH)

    beside = jnp.where(col > 0, 1, 0) + jnp.where(col < cols - 1, 1, 0)
    pl.semaphore_wait(barrier, rows - 1 + beside)

    def block_of(index):
        return pl.ds(pl.multiple_of(index * cap, cap), cap)

    cot_copies = [
        pltpu.make_async_remote_copy(
            src_ref=cot_hbm.at[block_of(peers[shift])],
            dst_ref=incoming.at[block_of(row)],
            send_sem=cot_send_sem.at[shift],
            recv_sem=cot_recv_sem.at[shift],
            device_id=(group, peers[shift], col),
            device_id_type=MESH,
        )
        for shift in range(1, rows)
    ]
    for copy in cot_copies:
        copy.start()
    own_cot = pltpu.make_async_copy(
        cot_hbm.at[block_of(row)], incoming.at[block_of(row)], own_sem.at[0]
    )
    own_cot.start()

    for side, (exists, _) in enumerate(near):

        @pl.when(jnp.logical_not(exists))
        def _():
            kv_far[side] = jnp.zeros(kv_far.shape[1:], BF16)
            dkv_far[side] = jnp.zeros(dkv_far.shape[1:], BF16)

    pick = (
        lax.broadcasted_iota(jnp.int32, (patch_count, keep), 0) == keep_ref[...]
    ).astype(F32).astype(BF16)
    loads[0].wait()
    for at, size in tiles(depth):
        kept[:, at : at + size] = dot(pick, patches[:, at : at + size], TN).astype(BF16)

    values = kept[...].astype(F32)
    centred = values - jnp.mean(values, axis=-1, keepdims=True)
    inv = lax.rsqrt(jnp.mean(centred * centred, axis=-1, keepdims=True) + 1e-06)
    inv_std[...] = inv
    scaled[...] = centred * inv
    normed[...] = (scaled[...] * gain_ref[...][None, :]).astype(BF16)

    loads[1].wait()
    for at, size in tiles(3 * heads * hd):
        proj[:, at : at + size] = dot(normed[...], wqkv[at : at + size, :], NT)

    pieces = [None] * (2 * heads)
    for piece in range(3 * heads):
        part = proj[:, piece * hd : (piece + 1) * hd]
        if piece < 2 * heads:
            mean = jnp.sum(part * part, axis=-1, keepdims=True) * (1.0 / hd)
            inv = lax.rsqrt(mean + 1e-06)
            raw[piece, :, :hd] = part
            rms[piece] = inv
            part = (part * inv).astype(BF16)
        else:
            part = part.astype(BF16)
        if piece < heads:
            qh[piece] = jnp.zeros(qh.shape[1:], BF16)
            qh[piece, :, :hd] = part
        else:
            which, head = divmod(piece - heads, heads)
            pieces[2 * head + which] = part
            kvh[0, 2 * head + which] = jnp.zeros(kvh.shape[2:], BF16)
            kvh[0, 2 * head + which, :, :hd] = part
    kv_send[...] = jnp.concatenate(pieces, axis=1)

    def side_copy(part, source, target_buffer, send_sems, recv_sems, bounds, side, slot):
        low, high = bounds[part]
        return pltpu.make_async_remote_copy(
            src_ref=source.at[:, low:high],
            dst_ref=target_buffer.at[slot, :, low:high],
            send_sem=send_sems.at[part, side],
            recv_sem=recv_sems.at[part, slot],
            device_id=near[side][1],
            device_id_type=MESH,
        )

    kv_cuts = cuts(heads, hd, True)
    dkv_cuts = cuts(heads, hd, False)

    def kv_copy(part, side, slot):
        return side_copy(part, kv_send, kv_far, kv_send_sem, kv_recv_sem, kv_cuts, side, slot)

    def dkv_copy(part, side, slot):
        return side_copy(
            part, dkv_send.at[side], dkv_far, dkv_send_sem, dkv_recv_sem, dkv_cuts, side, slot
        )

    for part in range(PARTS):
        for side, (exists, _) in enumerate(near):

            @pl.when(exists)
            def _():
                kv_copy(part, side, opposite[side]).start()

    slot_pick = (
        lax.broadcasted_iota(jnp.int32, (keep, keep), 0) == dest_ref[...]
    ).astype(F32).astype(BF16)
    for copy in cot_copies:
        copy.wait()
    own_cot.wait()
    for at, size in tiles(depth):
        token[:, at : at + size] = dot(slot_pick, incoming[:, at : at + size], TN).astype(BF16)
    loads[2].wait()
    out_grad = dot(token[...], wout[...], NT).astype(BF16)
    for head in range(heads):
        doh[head] = jnp.zeros(doh.shape[1:], BF16)
        doh[head, :, :hd] = out_grad[:, head * hd : (head + 1) * hd]

    above_row = jnp.maximum(row - 1, 0)
    below_row = jnp.minimum(row + 1, rows - 1)
    left_col = jnp.maximum(col - 1, 0)
    right_col = jnp.minimum(col + 1, cols - 1)
    limits = [
        counts_ref[row, col],
        jnp.where(row > 0, counts_ref[above_row, col] * link_ref[above_row, 1, col], 0),
        jnp.where(row < rows - 1, counts_ref[below_row, col] * link_ref[row, 1, col], 0),
        jnp.where(col > 0, counts_ref[row, left_col] * link_ref[row, 0, left_col], 0),
        jnp.where(col < cols - 1, counts_ref[row, right_col] * link_ref[row, 0, col], 0),
    ]

    panels = 5
    key_at = lax.broadcasted_iota(jnp.int32, (keep, keep), 0)

    def head_step(head, carry):
        coef = scale_ref[head] * (1.0 / math.sqrt(hd))
        query = qh[head]
        grad = doh[head]
        total = jnp.zeros((1, keep), F32)
        for panel in range(panels):
            scores = dot(kvh[panel, 2 * head], query, NT) * coef
            raised = jnp.where(key_at < limits[panel], jnp.exp(scores), 0.0)
            total = total + jnp.sum(raised, axis=0, keepdims=True)
            exps[panel] = raised
        inverse = 1.0 / total
        delta = jnp.zeros((1, keep), F32)
        attended = jnp.zeros((LANES, keep), F32)
        for panel in range(panels):
            value = kvh[panel, 2 * head + 1]
            weights = exps[panel] * inverse
            exps[panel] = weights
            rounded = weights.astype(BF16)
            attended = attended + dot(value, rounded, TN)
            dot_grad = dot(value, grad, NT)
            dps[panel] = dot_grad
            delta = delta + jnp.sum(weights * dot_grad, axis=0, keepdims=True)
            value_grad = dot(rounded, grad, NN)
            if panel == 0:
                own_dkv[2 * head + 1] = value_grad
            else:
                far_dkv[panel - 1, 2 * head + 1] = value_grad.astype(BF16)
        att_t[pl.ds(pl.multiple_of(head * hd, 8), hd), :] = attended[:hd]
        query_grad = jnp.zeros((LANES, keep), F32)
        for panel in range(panels):
            score_grad = (exps[panel] * (dps[panel] - delta)).astype(BF16)
            query_grad = query_grad + dot(kvh[panel, 2 * head], score_grad, TN)
            key_grad = dot(score_grad, query, NN) * coef
            if panel == 0:
                own_dkv[2 * head] = key_grad
            else:
                far_dkv[panel - 1, 2 * head] = key_grad.astype(BF16)
        upstream = query_grad.T[:, :hd] * coef
        split = raw[head, :, :hd]
        inv = rms[head]
        inner = jnp.sum(upstream * split, axis=-1, keepdims=True) * (1.0 / hd)
        pgh[head, :, :hd] = (inv * (upstream - split * (inv * inv * inner))).astype(BF16)
        return carry

    for part in range(PARTS):
        first, last = heads * part // PARTS, heads * (part + 1) // PARTS
        for side, (exists, _) in enumerate(near):

            @pl.when(exists)
            def _():
                kv_copy(part, side, side).wait_recv()

            for piece in range(2 * first, 2 * last):
                kvh[1 + side, piece] = jnp.zeros(kvh.shape[2:], BF16)
                kvh[1 + side, piece, :, :hd] = kv_far[side, :, piece * hd : (piece + 1) * hd]
        lax.fori_loop(first, last, head_step, 0)
        low, high = dkv_cuts[part]
        for side, (exists, _) in enumerate(near):
            dkv_send[side, :, low:high] = jnp.concatenate(
                [
                    far_dkv[
                        side, piece, :, max(low - piece * hd, 0) : min(high - piece * hd, hd)
                    ]
                    for piece in range(low // hd, -(-high // hd))
                ],
                axis=1,
            )

            @pl.when(exists)
            def _():
                dkv_copy(part, side, opposite[side]).start()

    attended = att_t[...].astype(BF16)
    for at, size in tiles(depth):
        span = slice(at, at + size)
        kept_out = (kept[:, span].astype(F32) + dot(attended, wout[:, span], TN)).astype(BF16)
        outgoing[:, span] = dot(slot_pick, kept_out, NN).astype(BF16)
    out_copies = [
        pltpu.make_async_remote_copy(
            src_ref=outgoing.at[block_of(peers[shift])],
            dst_ref=layer_hbm.at[block_of(row)],
            send_sem=out_send_sem.at[shift],
            recv_sem=out_recv_sem.at[shift],
            device_id=(group, peers[shift], col),
            device_id_type=MESH,
        )
        for shift in range(1, rows)
    ]
    for copy in out_copies:
        copy.start()
    own_out = pltpu.make_async_copy(
        outgoing.at[block_of(row)], layer_hbm.at[block_of(row)], own_sem.at[1]
    )
    own_out.start()

    far_sum = proj
    done = 0
    for part in range(PARTS):
        for side, (exists, _) in enumerate(near):

            @pl.when(exists)
            def _():
                dkv_copy(part, side, side).wait_recv()

        low, high = dkv_cuts[part]
        for at, size in tiles(high - low):
            span = slice(low + at, low + at + size)
            far_sum[:, span] = (
                dkv_far[0, :, span].astype(F32)
                + dkv_far[1, :, span].astype(F32)
                + dkv_far[2, :, span].astype(F32)
                + dkv_far[3, :, span].astype(F32)
            )
        for piece in range(done, high // hd):
            head, which = divmod(piece, 2)
            upstream = own_dkv[piece, :, :hd] + far_sum[:, piece * hd : (piece + 1) * hd]
            if which == 0:
                split = raw[heads + head, :, :hd]
                inv = rms[heads + head]
                inner = jnp.sum(upstream * split, axis=-1, keepdims=True) * (1.0 / hd)
                upstream = inv * (upstream - split * (inv * inv * inner))
            pgh[heads * (1 + which) + head, :, :hd] = upstream.astype(BF16)
        done = high // hd
    pg[...] = jnp.concatenate([pgh[piece, :, :hd] for piece in range(3 * heads)], axis=1)

    gained = proj
    for at, size in tiles(depth):
        span = slice(at, at + size)
        gained[:, span] = dot(pg[...], wqkv[:, span], NN) * gain_ref[span][None, :]
    grads = gained[:, :depth]
    mean_grad = jnp.mean(grads, axis=-1, keepdims=True)
    mean_scaled = jnp.mean(grads * scaled[...], axis=-1, keepdims=True)
    grad_out[...] = (
        token[...].astype(F32) + inv_std[...] * (grads - mean_grad - scaled[...] * mean_scaled)
    ).astype(BF16)
    store = pltpu.make_async_copy(grad_out, grad_hbm, own_sem.at[2])
    store.start()
    for part in range(PARTS):
        for side, (exists, _) in enumerate(near):

            @pl.when(exists)
            def _():
                kv_copy(part, side, side).wait_send()
                dkv_copy(part, side, side).wait_send()

    for copy in out_copies:
        copy.wait()
    own_out.wait()
    store.wait()


def per_device(
    rows, cols,
    patches, keep_list, destination, counts, link_open, ln_gain, w_qkv, head_scale, w_out, cotangent,
):
    keep = keep_list.shape[2]
    patch_count, depth = patches.shape[2:]
    heads = head_scale.shape[0]
    width = w_out.shape[0]
    hd = width // heads
    sizes = (rows, cols, keep, depth, patch_count, heads, hd)
    hbm = pl.BlockSpec(memory_space=pl.ANY)
    vmem = pl.BlockSpec(memory_space=pltpu.VMEM)
    smem = pl.BlockSpec(memory_space=pltpu.SMEM)
    dma = pltpu.SemaphoreType.DMA
    scratch = [
        pltpu.VMEM((patch_count, depth), BF16),
        pltpu.VMEM((3 * width, depth), BF16),
        pltpu.VMEM((width, depth), BF16),
        pltpu.VMEM((keep, depth), BF16),
        pltpu.VMEM((keep, depth), BF16),
        pltpu.VMEM((keep, depth), BF16),
        pltpu.VMEM((keep, depth), F32),
        pltpu.VMEM((keep, 1), F32),
        pltpu.VMEM((keep, depth), BF16),
        pltpu.VMEM((keep, 3 * width), F32),
        pltpu.VMEM((2 * heads, keep, LANES), F32),
        pltpu.VMEM((2 * heads, keep, 1), F32),
        pltpu.VMEM((heads, keep, LANES), BF16),
        pltpu.VMEM((heads, keep, LANES), BF16),
        pltpu.VMEM((5, 2 * heads, keep, LANES), BF16),
        pltpu.VMEM((keep, 2 * width), BF16),
        pltpu.VMEM((4, keep, 2 * width), BF16),
        pltpu.VMEM((5, keep, keep), F32),
        pltpu.VMEM((5, keep, keep), F32),
        pltpu.VMEM((width, keep), F32),
        pltpu.VMEM((2 * heads, keep, LANES), F32),
        pltpu.VMEM((4, 2 * heads, keep, LANES), BF16),
        pltpu.VMEM((4, keep, 2 * width), BF16),
        pltpu.VMEM((4, keep, 2 * width), BF16),
        pltpu.VMEM((3 * heads, keep, LANES), BF16),
        pltpu.VMEM((keep, 3 * width), BF16),
        pltpu.VMEM((keep, depth), BF16),
        pltpu.VMEM((keep, depth), BF16),
        dma((3,)),
        dma((rows,)),
        dma((rows,)),
        dma((PARTS, 4)),
        dma((PARTS, 4)),
        dma((PARTS, 4)),
        dma((PARTS, 4)),
        dma((rows,)),
        dma((rows,)),
        dma((3,)),
    ]
    layer_out, patch_grad = pl.pallas_call(
        functools.partial(kernel, sizes),
        out_shape=(
            jax.ShapeDtypeStruct((keep, depth), BF16),
            jax.ShapeDtypeStruct((keep, depth), BF16),
        ),
        in_specs=[hbm, vmem, vmem, smem, smem, vmem, hbm, smem, hbm, hbm],
        out_specs=(hbm, hbm),
        scratch_shapes=scratch,
        compiler_params=pltpu.CompilerParams(
            collective_id=0, has_side_effects=True, vmem_limit_bytes=60 * 2**20
        ),
    )(
        patches[0, 0], keep_list[0], destination[0], counts, link_open.transpose(0, 2, 1), ln_gain, w_qkv.T,
        head_scale, w_out, cotangent[0, 0],
    )
    return (layer_out[None, None], patch_grad[None, None])


def solution(mesh):
    window = P(("groups", "row"), "col", None, None)
    slots = P(("groups", "row"), "col", None)
    placed = (
        window, slots, slots, P("groups", None), P("groups", None, None), P(), P(), P(), P(), window,
    )
    return jax.shard_map(
        functools.partial(per_device, mesh.shape["row"], mesh.shape["col"]),
        mesh=mesh,
        in_specs=placed,
        out_specs=(window, window),
        check_vma=False,
    )
```

```python
import functools
import math

import jax
import jax.numpy as jnp
from jax import lax
from jax.experimental import pallas as pl
from jax.experimental.pallas import tpu as pltpu
from jax.sharding import PartitionSpec as P

MESH = pl.DeviceIdType.MESH
BF16 = jnp.bfloat16
F32 = jnp.float32
LANES = 128
NN = (((1,), (0,)), ((), ()))
NT = (((1,), (1,)), ((), ()))
TN = (((0,), (0,)), ((), ()))


def dot(a, b, dims):
    return lax.dot_general(a, b, dims, preferred_element_type=F32)


PARTS = 4


def cuts(heads, hd, up):
    ends = [0]
    for part in range(1, PARTS + 1):
        columns = 2 * hd * (heads * part // PARTS)
        if part < PARTS:
            columns = (columns + (LANES - 1 if up else 0)) // LANES * LANES
        ends.append(columns)
    return list(zip(ends[:-1], ends[1:]))


def tiles(total, step=256):
    return [(at, min(step, total - at)) for at in range(0, total, step)]


def kernel(
    sizes,
    patches_hbm, keep_ref, dest_ref, counts_ref, link_ref, gain_ref, wqkv_hbm, scale_ref, wout_hbm,
    cot_hbm,
    layer_hbm, grad_hbm,
    patches, wqkv, wout, incoming, kept, token, scaled, inv_std, normed, proj, raw, rms, qh, doh, kvh,
    kv_send, kv_far, exps, dps, att_t, own_dkv, far_dkv, dkv_send, dkv_far, pgh, pg, outgoing, grad_out,
    load_sem, cot_send_sem, cot_recv_sem, kv_send_sem, kv_recv_sem, dkv_send_sem, dkv_recv_sem,
    out_send_sem, out_recv_sem, own_sem,
):
    rows, cols, keep, depth, patch_count, heads, hd = sizes
    cap = keep // rows
    group = lax.axis_index("groups")
    row = lax.axis_index("row")
    col = lax.axis_index("col")

    loads = [
        pltpu.make_async_copy(patches_hbm, patches, load_sem.at[0]),
        pltpu.make_async_copy(wqkv_hbm, wqkv, load_sem.at[1]),
        pltpu.make_async_copy(wout_hbm, wout, load_sem.at[2]),
    ]
    for load in loads:
        load.start()

    near = [
        (row > 0, (group, row - 1, col)),
        (row < rows - 1, (group, row + 1, col)),
        (col > 0, (group, row, col - 1)),
        (col < cols - 1, (group, row, col + 1)),
    ]
    opposite = [1, 0, 3, 2]
    peers = [lax.rem(row + shift, rows) for shift in range(rows)]

    barrier = pltpu.get_barrier_semaphore()
    for shift in range(1, rows):
        pl.semaphore_signal(
            barrier, inc=1, device_id=(group, peers[shift], col), device_id_type=MESH
        )
    for exists, target in near[2:]:

        @pl.when(exists)
        def _():
            pl.semaphore_signal(barrier, inc=1, device_id=target, device_id_type=MESH)

    beside = jnp.where(col > 0, 1, 0) + jnp.where(col < cols - 1, 1, 0)
    pl.semaphore_wait(barrier, rows - 1 + beside)

    def block_of(index):
        return pl.ds(pl.multiple_of(index * cap, cap), cap)

    cot_copies = [
        pltpu.make_async_remote_copy(
            src_ref=cot_hbm.at[block_of(peers[shift])],
            dst_ref=incoming.at[block_of(row)],
            send_sem=cot_send_sem.at[shift],
            recv_sem=cot_recv_sem.at[shift],
            device_id=(group, peers[shift], col),
            device_id_type=MESH,
        )
        for shift in range(1, rows)
    ]
    for copy in cot_copies:
        copy.start()
    own_cot = pltpu.make_async_copy(
        cot_hbm.at[block_of(row)], incoming.at[block_of(row)], own_sem.at[0]
    )
    own_cot.start()

    for side, (exists, _) in enumerate(near):

        @pl.when(jnp.logical_not(exists))
        def _():
            kv_far[side] = jnp.zeros(kv_far.shape[1:], BF16)
            dkv_far[side] = jnp.zeros(dkv_far.shape[1:], BF16)

    pick = (
        lax.broadcasted_iota(jnp.int32, (patch_count, keep), 0) == keep_ref[...]
    ).astype(F32).astype(BF16)
    loads[0].wait()
    for at, size in tiles(depth):
        kept[:, at : at + size] = dot(pick, patches[:, at : at + size], TN).astype(BF16)

    values = kept[...].astype(F32)
    centred = values - jnp.mean(values, axis=-1, keepdims=True)
    inv = lax.rsqrt(jnp.mean(centred * centred, axis=-1, keepdims=True) + 1e-06)
    inv_std[...] = inv
    scaled[...] = centred * inv
    normed[...] = (scaled[...] * gain_ref[...][None, :]).astype(BF16)

    loads[1].wait()
    first_lane = heads * hd // LANES * LANES
    for at, size in tiles(3 * heads * hd - first_lane):
        span = slice(first_lane + at, first_lane + at + size)
        proj[:, span] = dot(normed[...], wqkv[span, :], NT)

    pieces = [None] * (2 * heads)
    for piece in range(heads, 3 * heads):
        part = proj[:, piece * hd : (piece + 1) * hd]
        if piece < 2 * heads:
            mean = jnp.sum(part * part, axis=-1, keepdims=True) * (1.0 / hd)
            inv = lax.rsqrt(mean + 1e-06)
            raw[piece, :, :hd] = part
            rms[piece] = inv
            part = (part * inv).astype(BF16)
        else:
            part = part.astype(BF16)
        which, head = divmod(piece - heads, heads)
        pieces[2 * head + which] = part
        kvh[0, 2 * head + which] = jnp.zeros(kvh.shape[2:], BF16)
        kvh[0, 2 * head + which, :, :hd] = part
    kv_send[...] = jnp.concatenate(pieces, axis=1)

    def side_copy(part, source, target_buffer, send_sems, recv_sems, bounds, side, slot):
        low, high = bounds[part]
        return pltpu.make_async_remote_copy(
            src_ref=source.at[:, low:high],
            dst_ref=target_buffer.at[slot, :, low:high],
            send_sem=send_sems.at[part, side],
            recv_sem=recv_sems.at[part, slot],
            device_id=near[side][1],
            device_id_type=MESH,
        )

    kv_cuts = cuts(heads, hd, True)
    dkv_cuts = cuts(heads, hd, False)

    def kv_copy(part, side, slot):
        return side_copy(part, kv_send, kv_far, kv_send_sem, kv_recv_sem, kv_cuts, side, slot)

    def dkv_copy(part, side, slot):
        return side_copy(
            part, dkv_send.at[side], dkv_far, dkv_send_sem, dkv_recv_sem, dkv_cuts, side, slot
        )

    for part in range(PARTS):
        for side, (exists, _) in enumerate(near):

            @pl.when(exists)
            def _():
                kv_copy(part, side, opposite[side]).start()

    for at, size in tiles(first_lane):
        proj[:, at : at + size] = dot(normed[...], wqkv[at : at + size, :], NT)
    for piece in range(heads):
        part = proj[:, piece * hd : (piece + 1) * hd]
        inv = lax.rsqrt(jnp.sum(part * part, axis=-1, keepdims=True) * (1.0 / hd) + 1e-06)
        raw[piece, :, :hd] = part
        rms[piece] = inv
        qh[piece] = jnp.zeros(qh.shape[1:], BF16)
        qh[piece, :, :hd] = (part * inv).astype(BF16)

    slot_pick = (
        lax.broadcasted_iota(jnp.int32, (keep, keep), 0) == dest_ref[...]
    ).astype(F32).astype(BF16)
    for copy in cot_copies:
        copy.wait()
    own_cot.wait()
    for at, size in tiles(depth):
        token[:, at : at + size] = dot(slot_pick, incoming[:, at : at + size], TN).astype(BF16)
    loads[2].wait()
    out_grad = dot(token[...], wout[...], NT).astype(BF16)
    for head in range(heads):
        doh[head] = jnp.zeros(doh.shape[1:], BF16)
        doh[head, :, :hd] = out_grad[:, head * hd : (head + 1) * hd]

    above_row = jnp.maximum(row - 1, 0)
    below_row = jnp.minimum(row + 1, rows - 1)
    left_col = jnp.maximum(col - 1, 0)
    right_col = jnp.minimum(col + 1, cols - 1)
    limits = [
        counts_ref[row, col],
        jnp.where(row > 0, counts_ref[above_row, col] * link_ref[above_row, 1, col], 0),
        jnp.where(row < rows - 1, counts_ref[below_row, col] * link_ref[row, 1, col], 0),
        jnp.where(col > 0, counts_ref[row, left_col] * link_ref[row, 0, left_col], 0),
        jnp.where(col < cols - 1, counts_ref[row, right_col] * link_ref[row, 0, col], 0),
    ]

    panels = 5
    key_at = lax.broadcasted_iota(jnp.int32, (keep, keep), 0)

    def head_step(head, carry):
        coef = scale_ref[head] * (1.0 / math.sqrt(hd))
        query = qh[head]
        grad = doh[head]
        total = jnp.zeros((1, keep), F32)
        for panel in range(panels):
            scores = dot(kvh[panel, 2 * head], query, NT) * coef
            raised = jnp.where(key_at < limits[panel], jnp.exp(scores), 0.0)
            total = total + jnp.sum(raised, axis=0, keepdims=True)
            exps[panel] = raised
        inverse = 1.0 / total
        delta = jnp.zeros((1, keep), F32)
        attended = jnp.zeros((LANES, keep), F32)
        for panel in range(panels):
            value = kvh[panel, 2 * head + 1]
            weights = exps[panel] * inverse
            exps[panel] = weights
            rounded = weights.astype(BF16)
            attended = attended + dot(value, rounded, TN)
            dot_grad = dot(value, grad, NT)
            dps[panel] = dot_grad
            delta = delta + jnp.sum(weights * dot_grad, axis=0, keepdims=True)
            value_grad = dot(rounded, grad, NN)
            if panel == 0:
                own_dkv[2 * head + 1] = value_grad
            else:
                far_dkv[panel - 1, 2 * head + 1] = value_grad.astype(BF16)
        att_t[pl.ds(pl.multiple_of(head * hd, 8), hd), :] = attended[:hd]
        query_grad = jnp.zeros((LANES, keep), F32)
        for panel in range(panels):
            score_grad = (exps[panel] * (dps[panel] - delta)).astype(BF16)
            query_grad = query_grad + dot(kvh[panel, 2 * head], score_grad, TN)
            key_grad = dot(score_grad, query, NN) * coef
            if panel == 0:
                own_dkv[2 * head] = key_grad
            else:
                far_dkv[panel - 1, 2 * head] = key_grad.astype(BF16)
        upstream = query_grad.T[:, :hd] * coef
        split = raw[head, :, :hd]
        inv = rms[head]
        inner = jnp.sum(upstream * split, axis=-1, keepdims=True) * (1.0 / hd)
        pgh[head, :, :hd] = (inv * (upstream - split * (inv * inv * inner))).astype(BF16)
        return carry

    for part in range(PARTS):
        first, last = heads * part // PARTS, heads * (part + 1) // PARTS
        for side, (exists, _) in enumerate(near):

            @pl.when(exists)
            def _():
                kv_copy(part, side, side).wait_recv()

            for piece in range(2 * first, 2 * last):
                kvh[1 + side, piece] = jnp.zeros(kvh.shape[2:], BF16)
                kvh[1 + side, piece, :, :hd] = kv_far[side, :, piece * hd : (piece + 1) * hd]
        lax.fori_loop(first, last, head_step, 0)
        low, high = dkv_cuts[part]
        for side, (exists, _) in enumerate(near):
            dkv_send[side, :, low:high] = jnp.concatenate(
                [
                    far_dkv[
                        side, piece, :, max(low - piece * hd, 0) : min(high - piece * hd, hd)
                    ]
                    for piece in range(low // hd, -(-high // hd))
                ],
                axis=1,
            )

            @pl.when(exists)
            def _():
                dkv_copy(part, side, opposite[side]).start()

    attended = att_t[...].astype(BF16)
    for at, size in tiles(depth):
        span = slice(at, at + size)
        kept_out = (kept[:, span].astype(F32) + dot(attended, wout[:, span], TN)).astype(BF16)
        outgoing[:, span] = dot(slot_pick, kept_out, NN).astype(BF16)
    out_copies = [
        pltpu.make_async_remote_copy(
            src_ref=outgoing.at[block_of(peers[shift])],
            dst_ref=layer_hbm.at[block_of(row)],
            send_sem=out_send_sem.at[shift],
            recv_sem=out_recv_sem.at[shift],
            device_id=(group, peers[shift], col),
            device_id_type=MESH,
        )
        for shift in range(1, rows)
    ]
    for copy in out_copies:
        copy.start()
    own_out = pltpu.make_async_copy(
        outgoing.at[block_of(row)], layer_hbm.at[block_of(row)], own_sem.at[1]
    )
    own_out.start()

    far_sum = proj
    done = 0
    for part in range(PARTS):
        for side, (exists, _) in enumerate(near):

            @pl.when(exists)
            def _():
                dkv_copy(part, side, side).wait_recv()

        low, high = dkv_cuts[part]
        for at, size in tiles(high - low):
            span = slice(low + at, low + at + size)
            far_sum[:, span] = (
                dkv_far[0, :, span].astype(F32)
                + dkv_far[1, :, span].astype(F32)
                + dkv_far[2, :, span].astype(F32)
                + dkv_far[3, :, span].astype(F32)
            )
        for piece in range(done, high // hd):
            head, which = divmod(piece, 2)
            upstream = own_dkv[piece, :, :hd] + far_sum[:, piece * hd : (piece + 1) * hd]
            if which == 0:
                split = raw[heads + head, :, :hd]
                inv = rms[heads + head]
                inner = jnp.sum(upstream * split, axis=-1, keepdims=True) * (1.0 / hd)
                upstream = inv * (upstream - split * (inv * inv * inner))
            pgh[heads * (1 + which) + head, :, :hd] = upstream.astype(BF16)
        done = high // hd
    pg[...] = jnp.concatenate([pgh[piece, :, :hd] for piece in range(3 * heads)], axis=1)

    gained = proj
    for at, size in tiles(depth):
        span = slice(at, at + size)
        gained[:, span] = dot(pg[...], wqkv[:, span], NN) * gain_ref[span][None, :]
    grads = gained[:, :depth]
    mean_grad = jnp.mean(grads, axis=-1, keepdims=True)
    mean_scaled = jnp.mean(grads * scaled[...], axis=-1, keepdims=True)
    grad_out[...] = (
        token[...].astype(F32) + inv_std[...] * (grads - mean_grad - scaled[...] * mean_scaled)
    ).astype(BF16)
    store = pltpu.make_async_copy(grad_out, grad_hbm, own_sem.at[2])
    store.start()
    for part in range(PARTS):
        for side, (exists, _) in enumerate(near):

            @pl.when(exists)
            def _():
                kv_copy(part, side, side).wait_send()
                dkv_copy(part, side, side).wait_send()

    for copy in out_copies:
        copy.wait()
    own_out.wait()
    store.wait()


def per_device(
    rows, cols,
    patches, keep_list, destination, counts, link_open, ln_gain, w_qkv, head_scale, w_out, cotangent,
):
    keep = keep_list.shape[2]
    patch_count, depth = patches.shape[2:]
    heads = head_scale.shape[0]
    width = w_out.shape[0]
    hd = width // heads
    sizes = (rows, cols, keep, depth, patch_count, heads, hd)
    hbm = pl.BlockSpec(memory_space=pl.ANY)
    vmem = pl.BlockSpec(memory_space=pltpu.VMEM)
    smem = pl.BlockSpec(memory_space=pltpu.SMEM)
    dma = pltpu.SemaphoreType.DMA
    scratch = [
        pltpu.VMEM((patch_count, depth), BF16),
        pltpu.VMEM((3 * width, depth), BF16),
        pltpu.VMEM((width, depth), BF16),
        pltpu.VMEM((keep, depth), BF16),
        pltpu.VMEM((keep, depth), BF16),
        pltpu.VMEM((keep, depth), BF16),
        pltpu.VMEM((keep, depth), F32),
        pltpu.VMEM((keep, 1), F32),
        pltpu.VMEM((keep, depth), BF16),
        pltpu.VMEM((keep, 3 * width), F32),
        pltpu.VMEM((2 * heads, keep, LANES), F32),
        pltpu.VMEM((2 * heads, keep, 1), F32),
        pltpu.VMEM((heads, keep, LANES), BF16),
        pltpu.VMEM((heads, keep, LANES), BF16),
        pltpu.VMEM((5, 2 * heads, keep, LANES), BF16),
        pltpu.VMEM((keep, 2 * width), BF16),
        pltpu.VMEM((4, keep, 2 * width), BF16),
        pltpu.VMEM((5, keep, keep), F32),
        pltpu.VMEM((5, keep, keep), F32),
        pltpu.VMEM((width, keep), F32),
        pltpu.VMEM((2 * heads, keep, LANES), F32),
        pltpu.VMEM((4, 2 * heads, keep, LANES), BF16),
        pltpu.VMEM((4, keep, 2 * width), BF16),
        pltpu.VMEM((4, keep, 2 * width), BF16),
        pltpu.VMEM((3 * heads, keep, LANES), BF16),
        pltpu.VMEM((keep, 3 * width), BF16),
        pltpu.VMEM((keep, depth), BF16),
        pltpu.VMEM((keep, depth), BF16),
        dma((3,)),
        dma((rows,)),
        dma((rows,)),
        dma((PARTS, 4)),
        dma((PARTS, 4)),
        dma((PARTS, 4)),
        dma((PARTS, 4)),
        dma((rows,)),
        dma((rows,)),
        dma((3,)),
    ]
    layer_out, patch_grad = pl.pallas_call(
        functools.partial(kernel, sizes),
        out_shape=(
            jax.ShapeDtypeStruct((keep, depth), BF16),
            jax.ShapeDtypeStruct((keep, depth), BF16),
        ),
        in_specs=[hbm, vmem, vmem, smem, smem, vmem, hbm, smem, hbm, hbm],
        out_specs=(hbm, hbm),
        scratch_shapes=scratch,
        compiler_params=pltpu.CompilerParams(
            collective_id=0, has_side_effects=True, vmem_limit_bytes=60 * 2**20
        ),
    )(
        patches[0, 0], keep_list[0], destination[0], counts, link_open.transpose(0, 2, 1), ln_gain, w_qkv.T,
        head_scale, w_out, cotangent[0, 0],
    )
    return (layer_out[None, None], patch_grad[None, None])


def solution(mesh):
    window = P(("groups", "row"), "col", None, None)
    slots = P(("groups", "row"), "col", None)
    placed = (
        window, slots, slots, P("groups", None), P("groups", None, None), P(), P(), P(), P(), window,
    )
    return jax.shard_map(
        functools.partial(per_device, mesh.shape["row"], mesh.shape["col"]),
        mesh=mesh,
        in_specs=placed,
        out_specs=(window, window),
        check_vma=False,
    )
```
